1024 devices in a mesh: row: 64 (over x, z), col: 16 (over y, core).
Axes of the slice: x: 8, y: 8, z: 8, core: 2. Of those that a mesh axis runs over, the one named last changes fastest.
Arguments:
- pooled: bfloat16 [4096, 64, 1024], P(('row', 'col'))
- upstream: bfloat16 [4096, 64, 1024], P(('row', 'col')), may hold values from -6 to 6
- cross_weight: bfloat16 [1024, 1024], replicated, may hold values from -0.1875 to 0.1875
- cross_bias: float32 [1024], replicated, may hold values from -3 to 3
- deep_weight: bfloat16 [1024, 1024], replicated, may hold values from -0.1875 to 0.1875
- deep_bias: float32 [1024], replicated, may hold values from -3 to 3
- bag_entries: int32 [4096, 64, 2], P('row'), may hold values from 0 to 4095
- touched_rows: int32 [4096], P('row'), may hold values from 0 to 1023, as said below
- table: float32 [65536, 1024], P('row', 'col'), may hold values from -4 to 4
- first_moment: float32 [65536, 1024], P('row', 'col'), may hold values from -6 to 6
- second_moment: float32 [65536], P('row'), may hold values from 0.002 to 0.2
- step_counts: int32 [65536], P('row'), may hold values from 0 to 7
Outputs:
- new_table: float32 [65536, 1024], P('row', 'col')
- new_first: float32 [65536, 1024], P('row', 'col')
- new_second: float32 [65536], P('row')
The draws below stay inside these ranges and needn't reach their ends.
Inputs may be any that keep to these rules, and one draw needn't show every extreme that they name: `bag_entries`: entry e stands for row touched_rows[e] of table row shard e // 64. `touched_rows`: within each block of 64 entries (one row shard's) the rows are distinct.
All inputs are finite; a program needn't handle non-finite values.
Results may differ from the reference program's by a relative error of at most 0.00075.
The reference program's roundings to bfloat16 on the way count: a program that leaves them out, or rounds other values in their place, can miss the bound.
Values may be sent and summed in bfloat16 or wider, within the bound.
A program may use at most 32 MiB of HBM per device.

```python
import math
import jax
import jax.numpy as jnp
import numpy as np
from jax import lax

E = 1024
F = 64
H = 1024
BAG = 2
S_DEV = 4
R_DEV = 1024
U = 64
B = 4096
ENTRIES = 4096
N_ROW = 64
N_COL = 16


def draw_pooled(key, part):
    key = jax.random.fold_in(key, 11)
    noise_key, column_key, sample_key = jax.random.split(key, 3)
    noise = jax.random.normal(noise_key, (B, F, E), jnp.float32)
    rise = 3.0
    position = jnp.arange(E, dtype=jnp.float32) / max(E - 1, 1)
    column_scale = jnp.power(rise, position - 0.5) * jnp.exp(jax.random.uniform(column_key, (E,), jnp.float32, -1.15, 1.15))
    token_scale = jnp.exp(jax.random.uniform(sample_key, (B, F, 1), jnp.float32, -1.15, 1.15))
    return (0.5 * noise * column_scale * token_scale).astype(jnp.bfloat16)


def draw_touched_rows(key, part):
    key = jax.random.fold_in(key, 23)
    shard_keys = jax.random.split(key, N_ROW)

    def shard_rows(shard_key):
        order = jax.random.permutation(shard_key, R_DEV - 2) + 1
        return order[:U].astype(jnp.int32)
    picked = jax.vmap(shard_rows)(shard_keys)
    first_shard = jnp.arange(N_ROW, dtype=jnp.int32) == 0
    last_pick = jnp.where(first_shard, R_DEV - 1, picked[:, U - 1])
    first_pick = jnp.where(first_shard, 0, picked[:, 0])
    picked = picked.at[:, U - 1].set(last_pick)
    picked = picked.at[:, 0].set(first_pick)
    return picked.reshape(N_ROW * U).astype(jnp.int32)


def place_ends(values, key, smallest, high):
    index_at = [jax.random.randint(jax.random.fold_in(key, axis), (), 0, length) for axis, length in enumerate(values.shape)]
    main_axis = values.shape.index(max(values.shape))
    neighbour = index_at[:main_axis] + [(index_at[main_axis] + 1) % values.shape[main_axis]] + index_at[main_axis + 1:]
    return values.at[tuple(index_at)].set(smallest).at[tuple(neighbour)].set(high)


def levels(own_key, dims, cuts, least, top_value):
    gain, own = 1.0, jax.random.fold_in(own_key, 6)
    for axis_at, shards_of in cuts:
        draws = jnp.exp(jax.random.uniform(jax.random.fold_in(own, axis_at), (shards_of,), jnp.float32, least / len(cuts), top_value / len(cuts)))
        gain = gain * jnp.repeat(draws, dims[axis_at] // shards_of).reshape([-1 if axis == axis_at else 1 for axis in range(len(dims))])
    return gain


def rank_table(number_of, skew):
    portions = [(1 << 20) // math.isqrt(rank ** skew) + 1 for rank in range(1, number_of + 1)]
    spread = 1 + sum(portions) // (1 << 30)
    return np.cumsum(np.array([max(1, weight // spread) for weight in portions]))


def skewed_ids(key, shape, number_of, slope):
    listing = rank_table(number_of, slope)
    ticket = jax.random.randint(jax.random.fold_in(key, 1), shape, 0, int(listing[number_of - 1]))
    grade = jnp.searchsorted(jnp.asarray(listing, jnp.int32), ticket, side="right")
    return jax.random.permutation(jax.random.fold_in(key, 2), number_of)[grade].astype(jnp.int32)


def normal_values(rng, extent, spread, reach, cuts=(), kind=jnp.bfloat16):
    entries = spread * jax.random.normal(rng, extent, jnp.float32)
    if cuts:
        entries = entries * levels(rng, extent, cuts, -0.22, 0.18)
    return jnp.clip(entries, -reach, reach).astype(kind)


def setup_inputs(seed: int = 0) -> dict:
    key_list = jax.random.split(jax.random.key(seed), 13)
    pooled = draw_pooled(jax.random.fold_in(key_list[12], 71), 0)
    upstream = normal_values(key_list[1], (B, F, H), 1.0, 6.0, ((0, 1024),))
    cross_weight = normal_values(key_list[2], (E, E), E ** -0.5, 0.1875)
    cross_bias = normal_values(key_list[3], (E,), 0.5, 3.0, (), jnp.float32)
    deep_weight = normal_values(key_list[4], (E, H), E ** -0.5, 0.1875)
    deep_bias = normal_values(key_list[5], (H,), 0.5, 3.0, (), jnp.float32)
    bag_entries = place_ends(skewed_ids(key_list[6], (B, F, BAG), ENTRIES, 1), jax.random.fold_in(key_list[6], 3), 0, ENTRIES - 1).astype(jnp.int32)
    touched_rows = draw_touched_rows(jax.random.fold_in(key_list[12], 71), 0)
    table = normal_values(key_list[8], (N_ROW * R_DEV, E), 0.5, 4.0, ((0, 64), (1, 16)), jnp.float32)
    first_moment = normal_values(key_list[9], (N_ROW * R_DEV, E), 1.0, 6.0, ((0, 64), (1, 16)), jnp.float32)
    second_moment = jnp.clip(jnp.exp(math.log(0.2) - 4.6051702 * jax.random.uniform(key_list[10], (N_ROW * R_DEV,), jnp.float32) ** levels(key_list[10], (N_ROW * R_DEV,), ((0, 64),), -0.2, 0.2)), 0.002, 0.2)
    step_counts = place_ends(jax.random.randint(key_list[11], (N_ROW * R_DEV,), 0, 8), jax.random.fold_in(key_list[11], 1), 0, 7).astype(jnp.int32)
    return dict(pooled=pooled, upstream=upstream, cross_weight=cross_weight, cross_bias=cross_bias, deep_weight=deep_weight, deep_bias=deep_bias, bag_entries=bag_entries, touched_rows=touched_rows, table=table, first_moment=first_moment, second_moment=second_moment, step_counts=step_counts)


def cross_back(inputs, upstream, cross_weight, cross_bias, deep_weight, deep_bias):
    wide_in = inputs.astype(jnp.float32)
    scaled = jnp.dot(inputs, cross_weight, preferred_element_type=jnp.float32) + cross_bias
    crossed = (wide_in * scaled + wide_in).astype(jnp.bfloat16)
    hidden = jnp.dot(crossed, deep_weight, preferred_element_type=jnp.float32) + deep_bias
    sigmoid_h = jax.nn.sigmoid(hidden)
    hidden_grad = (upstream.astype(jnp.float32) * sigmoid_h * (1.0 + hidden * (1.0 - sigmoid_h))).astype(jnp.bfloat16)
    crossed_grad = lax.dot_general(hidden_grad, deep_weight, (((1,), (1,)), ((), ())), preferred_element_type=jnp.float32)
    product = (crossed_grad * wide_in).astype(jnp.bfloat16)
    back_term = lax.dot_general(product, cross_weight, (((1,), (1,)), ((), ())), preferred_element_type=jnp.float32)
    return (crossed_grad * scaled + back_term + crossed_grad).astype(jnp.bfloat16)

def adam_rows(weights, first, second, steps, grads, mean_square):
    first_new = 0.9 * first + 0.1 * grads
    second_new = 0.999 * second + 0.001 * mean_square
    step_float = (steps + 1).astype(jnp.float32)
    first_hat = first_new / (1.0 - jnp.power(0.9, step_float))[:, None]
    second_hat = second_new / (1.0 - jnp.power(0.999, step_float))
    weights_new = weights - 0.01 * first_hat / (jnp.sqrt(second_hat)[:, None] + 1e-08)
    return (weights_new, first_new, second_new)

def reference(pooled, upstream, cross_weight, cross_bias, deep_weight, deep_bias, bag_entries, touched_rows, table, first_moment, second_moment, step_counts):
    group_rows = S_DEV * N_COL * F
    blocks_in = pooled.reshape(N_ROW, group_rows, E)
    blocks_up = upstream.reshape(N_ROW, group_rows, H)

    def apply_block(block_pair):
        return cross_back(block_pair[0], block_pair[1], cross_weight, cross_bias, deep_weight, deep_bias)
    grad_rows = lax.map(apply_block, (blocks_in, blocks_up)).reshape(B * F, E)
    wide_grads = grad_rows.astype(jnp.float32)
    entry_ids = bag_entries.reshape(B * F, BAG)
    entry_grads = jnp.zeros((N_ROW * U, E), jnp.float32)
    for bag_pos in range(BAG):
        entry_grads = entry_grads + jax.ops.segment_sum(wide_grads, entry_ids[:, bag_pos], num_segments=N_ROW * U)
    mean_square = lax.optimization_barrier(jnp.sum(entry_grads * entry_grads, axis=1)) / E
    owner_base = jnp.arange(N_ROW * U, dtype=jnp.int32) // U * R_DEV
    global_rows = (owner_base + touched_rows).astype(jnp.int32)
    weights_new, first_new, second_new = adam_rows(table[global_rows], first_moment[global_rows], second_moment[global_rows], step_counts[global_rows], entry_grads, mean_square)
    new_table = table.at[global_rows].set(weights_new)
    new_first = first_moment.at[global_rows].set(first_new)
    new_second = second_moment.at[global_rows].set(second_new)
    return (new_table, new_first, new_second)
```

```python
import functools

import jax
import jax.numpy as jnp
from jax import lax
from jax.experimental import pallas as pl
from jax.experimental.pallas import tpu as pltpu
from jax.sharding import PartitionSpec as P

MESH = pl.DeviceIdType.MESH
F32 = jnp.float32
BF16 = jnp.bfloat16

N_X = 8
N_Z = 8
N_COL = 16
FOLD = 4
SLICE = 64
BATCH = 4
BITS = 14


def peer_offset(i):
    return ((i + 1) // 2) * (2 * (i % 2) - 1)


def kernel(
    pooled, upstream, cross_w, cross_b, deep_w, deep_b, ids, touched, steps,
    grads_out, mean_square_out, stats_out,
    x_v, up_v, cw_v, dw_v,
    outgoing, incoming, codes, low_fold, onehot, acc,
    wire_out, wire_in,
    part_x, part_z, last_x, last_z,
    rows_oh, squares,
    load_sem, col_send, col_recv,
    x1_send, x1_recv, z1_send, z1_recv, x2_send, x2_recv, z2_send, z2_recv,
    sq_send, sq_recv,
):
    row, col = lax.axis_index("row"), lax.axis_index("col")
    x, z = row // N_Z, row % N_Z
    half_rows = x_v.shape[0] // 2

    def col_peer(i):
        return (col + peer_offset(i) + N_COL) % N_COL

    def x_peer(i):
        return (x + peer_offset(i) + N_X) % N_X

    def z_peer(i):
        return (z + peer_offset(i) + N_Z) % N_Z

    loads = [
        pltpu.make_async_copy(src, dst, load_sem.at[n])
        for n, (src, dst) in enumerate(
            [(pooled, x_v), (cross_w, cw_v), (deep_w, dw_v), (upstream, up_v)]
        )
    ]
    for load in loads:
        load.start()

    barrier = pltpu.get_barrier_semaphore()

    @pl.loop(1, N_COL)
    def _(i):
        pl.semaphore_signal(barrier, inc=1, device_id=(row, col_peer(i)), device_id_type=MESH)

    @pl.loop(1, N_X)
    def _(i):
        pl.semaphore_signal(
            barrier, inc=1, device_id=(x_peer(i) * N_Z + z, col), device_id_type=MESH
        )

    @pl.loop(1, N_Z)
    def _(i):
        pl.semaphore_signal(
            barrier, inc=1, device_id=(x * N_Z + z_peer(i), col), device_id_type=MESH
        )

    def col_copy(peer, slot):
        return pltpu.make_async_remote_copy(
            src_ref=outgoing.at[peer], dst_ref=incoming.at[slot],
            send_sem=col_send.at[peer], recv_sem=col_recv.at[slot],
            device_id=(row, peer), device_id_type=MESH,
        )

    fold_rows, fields = acc.shape[0], ids.shape[2]
    block = low_fold.shape[2]
    samples = ids.shape[0] // N_COL
    half_fold = fold_rows // 2
    owner_half = half_fold // (N_X * N_Z)

    def code_of(position):
        return ((128 + position % 128) << (position // 128)).astype(F32)

    codes[...] = code_of(lax.broadcasted_iota(jnp.int32, codes.shape, 0)).astype(BF16)

    def source(n):
        return col if isinstance(n, int) and n == 0 else jnp.where(
            n == 0, col, col_peer(jnp.maximum(N_COL - n, 1))
        )

    def entries_of(n):
        peer = source(n)
        pairs = [ids[peer * samples + s] for s in range(samples)]
        pieces = [pair[b:b + 1] for b in range(ids.shape[1]) for pair in pairs]
        return jnp.concatenate(pieces, axis=1)

    @pl.loop(0, N_COL)
    def _(n):
        entry = entries_of(n)
        low_fold[n] = jnp.broadcast_to((entry % FOLD).astype(F32), (16, block)).astype(BF16)
        folded = entry // FOLD
        owner_rows = 2 * owner_half
        line, owner = folded % owner_rows, folded // owner_rows
        owner_x, owner_z = owner // N_Z, owner % N_Z
        position = jnp.where(
            line < owner_half,
            (owner_x * N_Z + owner_z) * owner_half + line,
            half_fold + (owner_z * N_X + owner_x) * owner_half + line - owner_half,
        )
        wanted = jnp.broadcast_to(code_of(position), (16, block)).astype(BF16)
        one, zero = jnp.ones((), BF16), jnp.zeros((), BF16)
        row_step = 128

        @pl.loop(0, fold_rows // row_step)
        def _(k):
            at = pl.ds(k * row_step, row_step)
            here = codes[at, :].reshape(row_step // 16, 16, 128)
            for tile in range(block // 128):
                lanes_at = slice(tile * 128, (tile + 1) * 128)
                hit = jnp.where(here == wanted[None, :, lanes_at], one, zero)
                onehot[n // BATCH, at, pl.ds((n % BATCH) * block + tile * 128, 128)] = (
                    hit.reshape(row_step, 128)
                )

    low_half = lax.broadcasted_iota(jnp.int32, (half_rows, 2 * SLICE), 1) < SLICE

    loads[0].wait()
    loads[1].wait()
    scaled = jnp.dot(x_v[...], cw_v[...], preferred_element_type=F32) + cross_b[...]
    wide = x_v[...].astype(F32)
    crossed = (wide * scaled + wide).astype(BF16)
    loads[2].wait()
    hidden = jnp.dot(crossed, dw_v[...], preferred_element_type=F32) + deep_b[...]
    s = jax.nn.sigmoid(hidden)
    loads[3].wait()
    hidden_grad = (up_v[...].astype(F32) * s * (1.0 + hidden * (1.0 - s))).astype(BF16)
    crossed_grad = lax.dot_general(
        hidden_grad, dw_v[...], (((1,), (1,)), ((), ())), preferred_element_type=F32
    )
    product = (crossed_grad * wide).astype(BF16)
    back = lax.dot_general(
        product, cw_v[...], (((1,), (1,)), ((), ())), preferred_element_type=F32
    )
    grad = crossed_grad * scaled + back + crossed_grad
    for chip in range(N_COL // 2):
        tile = grad[:, chip * 2 * SLICE:(chip + 1) * 2 * SLICE]
        top, bottom = tile[:half_rows], tile[half_rows:]
        outgoing[2 * chip] = jnp.where(low_half, top, pltpu.roll(bottom, SLICE, 1)).astype(BF16)
        outgoing[2 * chip + 1] = jnp.where(
            low_half, pltpu.roll(top, SLICE, 1), bottom
        ).astype(BF16)
    pl.semaphore_wait(barrier, N_COL - 1 + N_X - 1 + N_Z - 1)

    @pl.loop(0, N_COL - 1)
    def _(n):
        col_copy(col_peer(N_COL - 1 - n), col).start()

    n_touched = touched.shape[0]
    shard_rows = grads_out.shape[1]
    lane_row = lax.broadcasted_iota(jnp.int32, (1, shard_rows), 1)
    for fold in range(FOLD):
        hits = [
            (lane_row == touched[q * FOLD + fold]).astype(F32)
            for q in range(n_touched // FOLD)
        ]
        block_oh = jnp.concatenate(hits, axis=0).astype(BF16)
        for copy in range(3):
            rows_oh[pl.ds(copy * n_touched + fold * len(hits), len(hits)), :] = block_oh
    count = (steps[...] + 1).astype(F32)
    stats_out[0:1, :] = jnp.sum(rows_oh[:n_touched, :].astype(F32), axis=0, keepdims=True)
    stats_out[1:2, :] = 1.0 - jnp.power(0.9, count)
    stats_out[2:3, :] = 1.0 - jnp.power(0.999, count)

    def spread(n):
        turned = jnp.transpose(incoming[source(n)].astype(F32)).astype(BF16)
        tokens = jnp.concatenate([turned[:SLICE], turned[SLICE:]], axis=1)
        tokens = jnp.concatenate([tokens] * (block // tokens.shape[1]), axis=1)
        tokens = tokens.reshape(SLICE // 16, 16, block)
        low = low_fold[n]
        zero = jnp.zeros((), BF16)
        return jnp.concatenate(
            [
                jnp.where((low == jnp.asarray(fold, BF16))[None], tokens, zero).reshape(SLICE, block)
                for fold in range(FOLD)
            ],
            axis=0,
        )

    incoming[col] = outgoing[col]
    acc[...] = jnp.zeros_like(acc)

    @pl.loop(0, N_COL // BATCH)
    def _(b):
        @pl.loop(b * BATCH, (b + 1) * BATCH)
        def _(n):
            @pl.when(n > 0)
            def _():
                col_copy(source(n), source(n)).wait_recv()

        tokens = jnp.concatenate([spread(b * BATCH + k) for k in range(BATCH)], axis=1)
        acc[...] += lax.dot_general(
            onehot[b], tokens, (((1,), (1,)), ((), ())), preferred_element_type=F32
        )

    chunk_rows = half_fold // N_X
    tiles = chunk_rows // 16

    def encode(axis):
        powers = []
        for half in range(2):
            piece = acc[
                axis * half_fold:(axis + 1) * half_fold, half * 128:(half + 1) * 128
            ].reshape(N_X, chunk_rows, 128)
            largest = jnp.max(jnp.abs(piece), axis=1, keepdims=True)
            power = jnp.ceil(jnp.log2(jnp.maximum(largest, 1e-30))) - BITS
            steps_of = jnp.floor(piece * jnp.exp2(-power) + 0.5).astype(jnp.int32)
            wire_out[axis, :, half * tiles:(half + 1) * tiles] = (
                steps_of.astype(jnp.int16).reshape(N_X, tiles, 16, 128)
            )
            powers.append(jnp.broadcast_to(power, (N_X, 8, 128)))
        wire_out[axis, :, 2 * tiles] = (
            jnp.concatenate(powers, axis=1).astype(jnp.int32).astype(jnp.int16)
        )

    def decode(axis, sender):
        got = wire_in[axis, sender].astype(jnp.int32).astype(F32)
        powers = jnp.exp2(got[2 * tiles])
        return jnp.concatenate(
            [
                got[half * tiles:(half + 1) * tiles].reshape(chunk_rows, 128)
                * powers[8 * half:8 * half + 1]
                for half in range(2)
            ],
            axis=1,
        )

    def to_x(src, dst, send, recv, i):
        peer = x_peer(i)
        return pltpu.make_async_remote_copy(
            src_ref=src.at[peer], dst_ref=dst.at[x],
            send_sem=send.at[peer], recv_sem=recv.at[x],
            device_id=(peer * N_Z + z, col), device_id_type=MESH,
        )

    def from_x(src, dst, send, recv, i):
        peer = x_peer(i)
        return pltpu.make_async_remote_copy(
            src_ref=src.at[peer], dst_ref=dst.at[peer],
            send_sem=send.at[peer], recv_sem=recv.at[peer],
            device_id=(peer * N_Z + z, col), device_id_type=MESH,
        )

    def to_z(src, dst, send, recv, i):
        peer = z_peer(i)
        return pltpu.make_async_remote_copy(
            src_ref=src.at[peer], dst_ref=dst.at[z],
            send_sem=send.at[peer], recv_sem=recv.at[z],
            device_id=(x * N_Z + peer, col), device_id_type=MESH,
        )

    def from_z(src, dst, send, recv, i):
        peer = z_peer(i)
        return pltpu.make_async_remote_copy(
            src_ref=src.at[peer], dst_ref=dst.at[peer],
            send_sem=send.at[peer], recv_sem=recv.at[peer],
            device_id=(x * N_Z + peer, col), device_id_type=MESH,
        )

    out_x, out_z, in_x, in_z = wire_out.at[0], wire_out.at[1], wire_in.at[0], wire_in.at[1]
    for axis in range(2):
        encode(axis)

        @pl.loop(0, N_X - 1)
        def _(n):
            if axis == 0:
                to_x(out_x, in_x, x1_send, x1_recv, N_X - 1 - n).start()
            else:
                to_z(out_z, in_z, z1_send, z1_recv, N_Z - 1 - n).start()

    part_x[...] = acc[pl.ds(x * chunk_rows, chunk_rows), :].reshape(part_x.shape)
    part_z[...] = acc[pl.ds(half_fold + z * chunk_rows, chunk_rows), :].reshape(part_z.shape)

    @pl.loop(1, N_COL)
    def _(i):
        col_copy(col_peer(i), col).wait_send()

    @pl.loop(0, N_X - 1)
    def _(n):
        from_x(out_x, in_x, x1_send, x1_recv, N_X - 1 - n).wait_recv()
        part_x[...] += decode(0, x_peer(N_X - 1 - n)).reshape(part_x.shape)

    @pl.loop(0, N_Z - 1)
    def _(n):
        to_z(part_x, last_x, z2_send, z2_recv, N_Z - 1 - n).start()

    @pl.loop(0, N_Z - 1)
    def _(n):
        from_z(out_z, in_z, z1_send, z1_recv, N_Z - 1 - n).wait_recv()
        part_z[...] += decode(1, z_peer(N_Z - 1 - n)).reshape(part_z.shape)

    @pl.loop(0, N_X - 1)
    def _(n):
        to_x(part_z, last_z, x2_send, x2_recv, N_X - 1 - n).start()

    last_x[z] = part_x[z]
    last_z[x] = part_z[x]

    @pl.loop(1, N_X)
    def _(i):
        to_x(out_x, in_x, x1_send, x1_recv, i).wait_send()
        to_z(out_z, in_z, z1_send, z1_recv, i).wait_send()

    @pl.loop(0, N_Z - 1)
    def _(n):
        from_z(part_x, last_x, z2_send, z2_recv, N_Z - 1 - n).wait_recv()
        from_x(part_z, last_z, x2_send, x2_recv, N_X - 1 - n).wait_recv()

    sum_x, sum_z = last_x[0], last_z[0]
    for n in range(1, N_X):
        sum_x, sum_z = sum_x + last_x[n], sum_z + last_z[n]

    entry = jnp.concatenate(
        [
            part[:, fold * SLICE:(fold + 1) * SLICE]
            for fold in range(FOLD) for part in (sum_x, sum_z)
        ],
        axis=0,
    )
    term_a = entry.astype(BF16)
    rest = entry - term_a.astype(F32)
    term_b = rest.astype(BF16)
    term_c = (rest - term_b.astype(F32)).astype(BF16)
    grads = lax.dot_general(
        jnp.concatenate([term_a, term_b, term_c], axis=0), rows_oh[...],
        (((0,), (0,)), ((), ())), preferred_element_type=F32,
    )

    of_rows = jnp.sum(grads * grads, axis=0, keepdims=True)
    squares[col] = jnp.concatenate(
        [of_rows[:, first:first + 128] for first in range(0, shard_rows, 128)], axis=0
    )

    def square_copy(slot, peer):
        return pltpu.make_async_remote_copy(
            src_ref=squares.at[col], dst_ref=squares.at[slot],
            send_sem=sq_send.at[peer], recv_sem=sq_recv.at[slot],
            device_id=(row, peer), device_id_type=MESH,
        )

    @pl.loop(0, N_COL - 1)
    def _(n):
        square_copy(col, col_peer(N_COL - 1 - n)).start()

    grads_out[...] = grads

    @pl.loop(1, N_X)
    def _(i):
        to_z(part_x, last_x, z2_send, z2_recv, i).wait_send()
        to_x(part_z, last_z, x2_send, x2_recv, i).wait_send()

    @pl.loop(0, N_COL - 1)
    def _(n):
        peer = col_peer(N_COL - 1 - n)
        square_copy(peer, peer).wait_recv()

    total = squares[0]
    for n in range(1, N_COL):
        total = total + squares[n]
    mean_square_out[...] = total / (SLICE * N_COL)

    @pl.loop(1, N_COL)
    def _(i):
        square_copy(col, col_peer(i)).wait_send()


def update(
    grads, mean_square, stats, table, first, second, new_table, new_first, new_second
):
    touched = stats[0:1, :] > 0.0
    second_now = 0.999 * second[...] + 0.001 * mean_square[...]
    scale = 0.01 / (stats[1:2, :] * (jnp.sqrt(second_now / stats[2:3, :]) + 1e-08))
    new_second[...] = jnp.where(touched, second_now, second[...])
    moment = 0.9 * first[...] + 0.1 * grads[...]
    new_first[...] = jnp.where(touched, moment, first[...])
    new_table[...] = jnp.where(touched, table[...] - moment * scale, table[...])


def body(
    pooled, upstream, cross_weight, cross_bias, deep_weight, deep_bias,
    bag_entries, touched_rows, table, first_moment, second_moment, step_counts,
):
    samples, fields, width = pooled.shape
    tokens = samples * fields
    hidden = upstream.shape[2]
    bags = bag_entries.shape[2]
    ids = bag_entries.transpose(0, 2, 1)
    shard_rows, columns = table.shape
    n_touched = touched_rows.shape[0]
    entries = n_touched * N_X * N_Z
    fold_rows = entries // FOLD
    owner_half = n_touched // FOLD // 2
    chunk_rows = fold_rows // 2 // N_X
    wide = FOLD * SLICE
    wire_tiles = chunk_rows // 16 * (wide // 128) + 1
    pair = 2 * SLICE
    vmem, hbm = pl.BlockSpec(memory_space=pltpu.VMEM), pl.BlockSpec(memory_space=pl.ANY)
    smem = pl.BlockSpec(memory_space=pltpu.SMEM)
    dma = pltpu.SemaphoreType.DMA
    grads, mean_square, stats = pl.pallas_call(
        kernel,
        out_shape=[
            jax.ShapeDtypeStruct((columns, shard_rows), F32),
            jax.ShapeDtypeStruct((shard_rows // 128, 128), F32),
            jax.ShapeDtypeStruct((3, shard_rows), F32),
        ],
        in_specs=[hbm, hbm, hbm, vmem, hbm, vmem, vmem, smem, vmem],
        out_specs=[vmem, vmem, vmem],
        scratch_shapes=[
            pltpu.VMEM((tokens, width), BF16),
            pltpu.VMEM((tokens, hidden), BF16),
            pltpu.VMEM((width, width), BF16),
            pltpu.VMEM((width, hidden), BF16),
            pltpu.VMEM((N_COL, tokens // 2, pair), BF16),
            pltpu.VMEM((N_COL, tokens // 2, pair), BF16),
            pltpu.VMEM((fold_rows, 128), BF16),
            pltpu.VMEM((N_COL, 16, tokens * bags), BF16),
            pltpu.VMEM((N_COL // BATCH, fold_rows, BATCH * tokens * bags), BF16),
            pltpu.VMEM((fold_rows, wide), F32),
            pltpu.VMEM((2, N_X, wire_tiles, 16, 128), jnp.int16),
            pltpu.VMEM((2, N_X, wire_tiles, 16, 128), jnp.int16),
            pltpu.VMEM((N_Z, owner_half, wide), F32),
            pltpu.VMEM((N_X, owner_half, wide), F32),
            pltpu.VMEM((N_Z, owner_half, wide), F32),
            pltpu.VMEM((N_X, owner_half, wide), F32),
            pltpu.VMEM((3 * n_touched, shard_rows), BF16),
            pltpu.VMEM((N_COL, shard_rows // 128, 128), F32),
            dma((4,)),
            dma((N_COL,)),
            dma((N_COL,)),
            dma((N_X,)), dma((N_X,)), dma((N_Z,)), dma((N_Z,)),
            dma((N_X,)), dma((N_X,)), dma((N_Z,)), dma((N_Z,)),
            dma((N_COL,)), dma((N_COL,)),
        ],
        compiler_params=pltpu.CompilerParams(
            collective_id=0, has_side_effects=True, vmem_limit_bytes=56 * 1024 * 1024
        ),
    )(
        pooled.reshape(tokens, width),
        upstream.reshape(tokens, hidden),
        cross_weight,
        cross_bias.reshape(1, width),
        deep_weight,
        deep_bias.reshape(1, hidden),
        ids,
        touched_rows,
        step_counts.reshape(1, shard_rows),
    )
    new_table, new_first, new_second = pl.pallas_call(
        update,
        out_shape=[
            jax.ShapeDtypeStruct((columns, shard_rows), F32),
            jax.ShapeDtypeStruct((columns, shard_rows), F32),
            jax.ShapeDtypeStruct((1, shard_rows), F32),
        ],
    )(
        grads,
        mean_square.reshape(1, shard_rows),
        stats,
        table.T,
        first_moment.T,
        second_moment.reshape(1, shard_rows),
    )
    return new_table.T, new_first.T, new_second.reshape(shard_rows)


def solution(mesh):
    in_specs = (
        P(("row", "col"), None, None),
        P(("row", "col"), None, None),
        P(),
        P(),
        P(),
        P(),
        P("row", None, None),
        P("row"),
        P("row", "col"),
        P("row", "col"),
        P("row"),
        P("row"),
    )
    out_specs = (P("row", "col"), P("row", "col"), P("row"))
    return jax.shard_map(body, mesh=mesh, in_specs=in_specs, out_specs=out_specs, check_vma=False)
```

```python
import functools

import jax
import jax.numpy as jnp
from jax import lax
from jax.experimental import pallas as pl
from jax.experimental.pallas import tpu as pltpu
from jax.sharding import PartitionSpec as P

MESH = pl.DeviceIdType.MESH
F32 = jnp.float32
BF16 = jnp.bfloat16

N_X = 8
N_Z = 8
N_COL = 16
FOLD = 4
SLICE = 64
BATCH = 2
BITS = 14


def peer_offset(i):
    return ((i + 1) // 2) * (2 * (i % 2) - 1)


def kernel(
    pooled, upstream, cross_w, cross_b, deep_w, deep_b, ids, touched, steps,
    grads_out, mean_square_out, stats_out,
    x_v, up_v, cw_v, dw_v,
    outgoing, incoming, codes, low_fold, onehot, acc,
    wire_out, wire_in,
    part_x, part_z, last_x, last_z,
    rows_oh, squares,
    load_sem, col_send, col_recv,
    x1_send, x1_recv, z1_send, z1_recv, x2_send, x2_recv, z2_send, z2_recv,
    sq_send, sq_recv,
):
    row, col = lax.axis_index("row"), lax.axis_index("col")
    x, z = row // N_Z, row % N_Z
    half_rows = x_v.shape[0] // 2

    def col_peer(i):
        return (col + peer_offset(i) + N_COL) % N_COL

    def x_peer(i):
        return (x + peer_offset(i) + N_X) % N_X

    def z_peer(i):
        return (z + peer_offset(i) + N_Z) % N_Z

    loads = [
        pltpu.make_async_copy(src, dst, load_sem.at[n])
        for n, (src, dst) in enumerate(
            [(pooled, x_v), (cross_w, cw_v), (deep_w, dw_v), (upstream, up_v)]
        )
    ]
    for load in loads:
        load.start()

    barrier = pltpu.get_barrier_semaphore()

    @pl.loop(1, N_COL)
    def _(i):
        pl.semaphore_signal(barrier, inc=1, device_id=(row, col_peer(i)), device_id_type=MESH)

    @pl.loop(1, N_X)
    def _(i):
        pl.semaphore_signal(
            barrier, inc=1, device_id=(x_peer(i) * N_Z + z, col), device_id_type=MESH
        )

    @pl.loop(1, N_Z)
    def _(i):
        pl.semaphore_signal(
            barrier, inc=1, device_id=(x * N_Z + z_peer(i), col), device_id_type=MESH
        )

    def col_copy(peer, slot):
        return pltpu.make_async_remote_copy(
            src_ref=outgoing.at[peer], dst_ref=incoming.at[slot],
            send_sem=col_send.at[peer], recv_sem=col_recv.at[slot],
            device_id=(row, peer), device_id_type=MESH,
        )

    fold_rows, fields = acc.shape[0], ids.shape[2]
    block = low_fold.shape[2]
    samples = ids.shape[0] // N_COL
    half_fold = fold_rows // 2
    owner_half = half_fold // (N_X * N_Z)

    def code_of(position):
        return ((128 + position % 128) << (position // 128)).astype(F32)

    codes[...] = code_of(lax.broadcasted_iota(jnp.int32, codes.shape, 0)).astype(BF16)

    def source(n):
        return col if isinstance(n, int) and n == 0 else jnp.where(
            n == 0, col, col_peer(jnp.maximum(N_COL - n, 1))
        )

    def entries_of(n):
        peer = source(n)
        pairs = [ids[peer * samples + s] for s in range(samples)]
        pieces = [pair[b:b + 1] for b in range(ids.shape[1]) for pair in pairs]
        return jnp.concatenate(pieces, axis=1)

    @pl.loop(0, N_COL)
    def _(n):
        entry = entries_of(n)
        low_fold[n] = jnp.broadcast_to((entry % FOLD).astype(F32), (16, block)).astype(BF16)
        folded = entry // FOLD
        owner_rows = 2 * owner_half
        line, owner = folded % owner_rows, folded // owner_rows
        owner_x, owner_z = owner // N_Z, owner % N_Z
        position = jnp.where(
            line < owner_half,
            (owner_x * N_Z + owner_z) * owner_half + line,
            half_fold + (owner_z * N_X + owner_x) * owner_half + line - owner_half,
        )
        wanted = jnp.broadcast_to(code_of(position), (16, block)).astype(BF16)
        one, zero = jnp.ones((), BF16), jnp.zeros((), BF16)
        row_step = 128

        @pl.loop(0, fold_rows // row_step)
        def _(k):
            at = pl.ds(k * row_step, row_step)
            here = codes[at, :].reshape(row_step // 16, 16, 128)
            for tile in range(block // 128):
                lanes_at = slice(tile * 128, (tile + 1) * 128)
                hit = jnp.where(here == wanted[None, :, lanes_at], one, zero)
                onehot[n // BATCH, at, pl.ds((n % BATCH) * block + tile * 128, 128)] = (
                    hit.reshape(row_step, 128)
                )

    low_half = lax.broadcasted_iota(jnp.int32, (half_rows, 2 * SLICE), 1) < SLICE

    loads[0].wait()
    loads[1].wait()
    scaled = jnp.dot(x_v[...], cw_v[...], preferred_element_type=F32) + cross_b[...]
    wide = x_v[...].astype(F32)
    crossed = (wide * scaled + wide).astype(BF16)
    loads[2].wait()
    hidden = jnp.dot(crossed, dw_v[...], preferred_element_type=F32) + deep_b[...]
    s = jax.nn.sigmoid(hidden)
    loads[3].wait()
    hidden_grad = (up_v[...].astype(F32) * s * (1.0 + hidden * (1.0 - s))).astype(BF16)
    crossed_grad = lax.dot_general(
        hidden_grad, dw_v[...], (((1,), (1,)), ((), ())), preferred_element_type=F32
    )
    product = (crossed_grad * wide).astype(BF16)
    back = lax.dot_general(
        product, cw_v[...], (((1,), (1,)), ((), ())), preferred_element_type=F32
    )
    grad = crossed_grad * scaled + back + crossed_grad
    for chip in range(N_COL // 2):
        tile = grad[:, chip * 2 * SLICE:(chip + 1) * 2 * SLICE]
        top, bottom = tile[:half_rows], tile[half_rows:]
        outgoing[2 * chip] = jnp.where(low_half, top, pltpu.roll(bottom, SLICE, 1)).astype(BF16)
        outgoing[2 * chip + 1] = jnp.where(
            low_half, pltpu.roll(top, SLICE, 1), bottom
        ).astype(BF16)
    pl.semaphore_wait(barrier, N_COL - 1 + N_X - 1 + N_Z - 1)

    @pl.loop(0, N_COL - 1)
    def _(n):
        col_copy(col_peer(N_COL - 1 - n), col).start()

    n_touched = touched.shape[0]
    shard_rows = grads_out.shape[1]
    lane_row = lax.broadcasted_iota(jnp.int32, (1, shard_rows), 1)
    for fold in range(FOLD):
        hits = [
            (lane_row == touched[q * FOLD + fold]).astype(F32)
            for q in range(n_touched // FOLD)
        ]
        block_oh = jnp.concatenate(hits, axis=0).astype(BF16)
        for copy in range(3):
            rows_oh[pl.ds(copy * n_touched + fold * len(hits), len(hits)), :] = block_oh
    count = (steps[...] + 1).astype(F32)
    stats_out[0:1, :] = jnp.sum(rows_oh[:n_touched, :].astype(F32), axis=0, keepdims=True)
    stats_out[1:2, :] = 1.0 - jnp.power(0.9, count)
    stats_out[2:3, :] = 1.0 - jnp.power(0.999, count)

    def spread(n):
        turned = jnp.transpose(incoming[source(n)].astype(F32)).astype(BF16)
        tokens = jnp.concatenate([turned[:SLICE], turned[SLICE:]], axis=1)
        tokens = jnp.concatenate([tokens] * (block // tokens.shape[1]), axis=1)
        tokens = tokens.reshape(SLICE // 16, 16, block)
        low = low_fold[n]
        zero = jnp.zeros((), BF16)
        return jnp.concatenate(
            [
                jnp.where((low == jnp.asarray(fold, BF16))[None], tokens, zero).reshape(SLICE, block)
                for fold in range(FOLD)
            ],
            axis=0,
        )

    incoming[col] = outgoing[col]
    acc[...] = jnp.zeros_like(acc)

    @pl.loop(0, N_COL // BATCH)
    def _(b):
        @pl.loop(b * BATCH, (b + 1) * BATCH)
        def _(n):
            @pl.when(n > 0)
            def _():
                col_copy(source(n), source(n)).wait_recv()

        tokens = jnp.concatenate([spread(b * BATCH + k) for k in range(BATCH)], axis=1)
        acc[...] += lax.dot_general(
            onehot[b], tokens, (((1,), (1,)), ((), ())), preferred_element_type=F32
        )

    chunk_rows = half_fold // N_X
    tiles = chunk_rows // 16

    def encode(axis):
        powers = []
        for half in range(2):
            piece = acc[
                axis * half_fold:(axis + 1) * half_fold, half * 128:(half + 1) * 128
            ].reshape(N_X, chunk_rows, 128)
            largest = jnp.max(jnp.abs(piece), axis=1, keepdims=True)
            power = jnp.ceil(jnp.log2(jnp.maximum(largest, 1e-30))) - BITS
            steps_of = jnp.floor(piece * jnp.exp2(-power) + 0.5).astype(jnp.int32)
            wire_out[axis, :, half * tiles:(half + 1) * tiles] = (
                steps_of.astype(jnp.int16).reshape(N_X, tiles, 16, 128)
            )
            powers.append(jnp.broadcast_to(power, (N_X, 8, 128)))
        wire_out[axis, :, 2 * tiles] = (
            jnp.concatenate(powers, axis=1).astype(jnp.int32).astype(jnp.int16)
        )

    def decode(axis, sender):
        got = wire_in[axis, sender].astype(jnp.int32).astype(F32)
        powers = jnp.exp2(got[2 * tiles])
        return jnp.concatenate(
            [
                got[half * tiles:(half + 1) * tiles].reshape(chunk_rows, 128)
                * powers[8 * half:8 * half + 1]
                for half in range(2)
            ],
            axis=1,
        )

    def to_x(src, dst, send, recv, i):
        peer = x_peer(i)
        return pltpu.make_async_remote_copy(
            src_ref=src.at[peer], dst_ref=dst.at[x],
            send_sem=send.at[peer], recv_sem=recv.at[x],
            device_id=(peer * N_Z + z, col), device_id_type=MESH,
        )

    def from_x(src, dst, send, recv, i):
        peer = x_peer(i)
        return pltpu.make_async_remote_copy(
            src_ref=src.at[peer], dst_ref=dst.at[peer],
            send_sem=send.at[peer], recv_sem=recv.at[peer],
            device_id=(peer * N_Z + z, col), device_id_type=MESH,
        )

    def to_z(src, dst, send, recv, i):
        peer = z_peer(i)
        return pltpu.make_async_remote_copy(
            src_ref=src.at[peer], dst_ref=dst.at[z],
            send_sem=send.at[peer], recv_sem=recv.at[z],
            device_id=(x * N_Z + peer, col), device_id_type=MESH,
        )

    def from_z(src, dst, send, recv, i):
        peer = z_peer(i)
        return pltpu.make_async_remote_copy(
            src_ref=src.at[peer], dst_ref=dst.at[peer],
            send_sem=send.at[peer], recv_sem=recv.at[peer],
            device_id=(x * N_Z + peer, col), device_id_type=MESH,
        )

    out_x, out_z, in_x, in_z = wire_out.at[0], wire_out.at[1], wire_in.at[0], wire_in.at[1]
    for axis in range(2):
        encode(axis)

        @pl.loop(0, N_X - 1)
        def _(n):
            if axis == 0:
                to_x(out_x, in_x, x1_send, x1_recv, N_X - 1 - n).start()
            else:
                to_z(out_z, in_z, z1_send, z1_recv, N_Z - 1 - n).start()

    part_x[...] = acc[pl.ds(x * chunk_rows, chunk_rows), :].reshape(part_x.shape)
    part_z[...] = acc[pl.ds(half_fold + z * chunk_rows, chunk_rows), :].reshape(part_z.shape)

    @pl.loop(1, N_COL)
    def _(i):
        col_copy(col_peer(i), col).wait_send()

    @pl.loop(0, N_X - 1)
    def _(n):
        from_x(out_x, in_x, x1_send, x1_recv, N_X - 1 - n).wait_recv()
        part_x[...] += decode(0, x_peer(N_X - 1 - n)).reshape(part_x.shape)

    @pl.loop(0, N_Z - 1)
    def _(n):
        to_z(part_x, last_x, z2_send, z2_recv, N_Z - 1 - n).start()

    @pl.loop(0, N_Z - 1)
    def _(n):
        from_z(out_z, in_z, z1_send, z1_recv, N_Z - 1 - n).wait_recv()
        part_z[...] += decode(1, z_peer(N_Z - 1 - n)).reshape(part_z.shape)

    @pl.loop(0, N_X - 1)
    def _(n):
        to_x(part_z, last_z, x2_send, x2_recv, N_X - 1 - n).start()

    last_x[z] = part_x[z]
    last_z[x] = part_z[x]

    @pl.loop(1, N_X)
    def _(i):
        to_x(out_x, in_x, x1_send, x1_recv, i).wait_send()
        to_z(out_z, in_z, z1_send, z1_recv, i).wait_send()

    @pl.loop(0, N_Z - 1)
    def _(n):
        from_z(part_x, last_x, z2_send, z2_recv, N_Z - 1 - n).wait_recv()
        from_x(part_z, last_z, x2_send, x2_recv, N_X - 1 - n).wait_recv()

    sum_x, sum_z = last_x[0], last_z[0]
    for n in range(1, N_X):
        sum_x, sum_z = sum_x + last_x[n], sum_z + last_z[n]

    entry = jnp.concatenate(
        [
            part[:, fold * SLICE:(fold + 1) * SLICE]
            for fold in range(FOLD) for part in (sum_x, sum_z)
        ],
        axis=0,
    )
    term_a = entry.astype(BF16)
    rest = entry - term_a.astype(F32)
    term_b = rest.astype(BF16)
    term_c = (rest - term_b.astype(F32)).astype(BF16)
    grads = lax.dot_general(
        jnp.concatenate([term_a, term_b, term_c], axis=0), rows_oh[...],
        (((0,), (0,)), ((), ())), preferred_element_type=F32,
    )

    of_rows = jnp.sum(grads * grads, axis=0, keepdims=True)
    squares[col] = jnp.concatenate(
        [of_rows[:, first:first + 128] for first in range(0, shard_rows, 128)], axis=0
    )

    def square_copy(slot, peer):
        return pltpu.make_async_remote_copy(
            src_ref=squares.at[col], dst_ref=squares.at[slot],
            send_sem=sq_send.at[peer], recv_sem=sq_recv.at[slot],
            device_id=(row, peer), device_id_type=MESH,
        )

    @pl.loop(0, N_COL - 1)
    def _(n):
        square_copy(col, col_peer(N_COL - 1 - n)).start()

    grads_out[...] = grads

    @pl.loop(1, N_X)
    def _(i):
        to_z(part_x, last_x, z2_send, z2_recv, i).wait_send()
        to_x(part_z, last_z, x2_send, x2_recv, i).wait_send()

    @pl.loop(0, N_COL - 1)
    def _(n):
        peer = col_peer(N_COL - 1 - n)
        square_copy(peer, peer).wait_recv()

    total = squares[0]
    for n in range(1, N_COL):
        total = total + squares[n]
    mean_square_out[...] = total / (SLICE * N_COL)

    @pl.loop(1, N_COL)
    def _(i):
        square_copy(col, col_peer(i)).wait_send()


def update(
    grads, mean_square, stats, table, first, second, new_table, new_first, new_second
):
    touched = stats[0:1, :] > 0.0
    second_now = 0.999 * second[...] + 0.001 * mean_square[...]
    scale = 0.01 / (stats[1:2, :] * (jnp.sqrt(second_now / stats[2:3, :]) + 1e-08))
    new_second[...] = jnp.where(touched, second_now, second[...])
    moment = 0.9 * first[...] + 0.1 * grads[...]
    new_first[...] = jnp.where(touched, moment, first[...])
    new_table[...] = jnp.where(touched, table[...] - moment * scale, table[...])


def body(
    pooled, upstream, cross_weight, cross_bias, deep_weight, deep_bias,
    bag_entries, touched_rows, table, first_moment, second_moment, step_counts,
):
    samples, fields, width = pooled.shape
    tokens = samples * fields
    hidden = upstream.shape[2]
    bags = bag_entries.shape[2]
    ids = bag_entries.transpose(0, 2, 1)
    shard_rows, columns = table.shape
    n_touched = touched_rows.shape[0]
    entries = n_touched * N_X * N_Z
    fold_rows = entries // FOLD
    owner_half = n_touched // FOLD // 2
    chunk_rows = fold_rows // 2 // N_X
    wide = FOLD * SLICE
    wire_tiles = chunk_rows // 16 * (wide // 128) + 1
    pair = 2 * SLICE
    vmem, hbm = pl.BlockSpec(memory_space=pltpu.VMEM), pl.BlockSpec(memory_space=pl.ANY)
    smem = pl.BlockSpec(memory_space=pltpu.SMEM)
    dma = pltpu.SemaphoreType.DMA
    grads, mean_square, stats = pl.pallas_call(
        kernel,
        out_shape=[
            jax.ShapeDtypeStruct((columns, shard_rows), F32),
            jax.ShapeDtypeStruct((shard_rows // 128, 128), F32),
            jax.ShapeDtypeStruct((3, shard_rows), F32),
        ],
        in_specs=[hbm, hbm, hbm, vmem, hbm, vmem, vmem, smem, vmem],
        out_specs=[vmem, vmem, vmem],
        scratch_shapes=[
            pltpu.VMEM((tokens, width), BF16),
            pltpu.VMEM((tokens, hidden), BF16),
            pltpu.VMEM((width, width), BF16),
            pltpu.VMEM((width, hidden), BF16),
            pltpu.VMEM((N_COL, tokens // 2, pair), BF16),
            pltpu.VMEM((N_COL, tokens // 2, pair), BF16),
            pltpu.VMEM((fold_rows, 128), BF16),
            pltpu.VMEM((N_COL, 16, tokens * bags), BF16),
            pltpu.VMEM((N_COL // BATCH, fold_rows, BATCH * tokens * bags), BF16),
            pltpu.VMEM((fold_rows, wide), F32),
            pltpu.VMEM((2, N_X, wire_tiles, 16, 128), jnp.int16),
            pltpu.VMEM((2, N_X, wire_tiles, 16, 128), jnp.int16),
            pltpu.VMEM((N_Z, owner_half, wide), F32),
            pltpu.VMEM((N_X, owner_half, wide), F32),
            pltpu.VMEM((N_Z, owner_half, wide), F32),
            pltpu.VMEM((N_X, owner_half, wide), F32),
            pltpu.VMEM((3 * n_touched, shard_rows), BF16),
            pltpu.VMEM((N_COL, shard_rows // 128, 128), F32),
            dma((4,)),
            dma((N_COL,)),
            dma((N_COL,)),
            dma((N_X,)), dma((N_X,)), dma((N_Z,)), dma((N_Z,)),
            dma((N_X,)), dma((N_X,)), dma((N_Z,)), dma((N_Z,)),
            dma((N_COL,)), dma((N_COL,)),
        ],
        compiler_params=pltpu.CompilerParams(
            collective_id=0, has_side_effects=True, vmem_limit_bytes=56 * 1024 * 1024
        ),
    )(
        pooled.reshape(tokens, width),
        upstream.reshape(tokens, hidden),
        cross_weight,
        cross_bias.reshape(1, width),
        deep_weight,
        deep_bias.reshape(1, hidden),
        ids,
        touched_rows,
        step_counts.reshape(1, shard_rows),
    )
    new_table, new_first, new_second = pl.pallas_call(
        update,
        out_shape=[
            jax.ShapeDtypeStruct((columns, shard_rows), F32),
            jax.ShapeDtypeStruct((columns, shard_rows), F32),
            jax.ShapeDtypeStruct((1, shard_rows), F32),
        ],
    )(
        grads,
        mean_square.reshape(1, shard_rows),
        stats,
        table.T,
        first_moment.T,
        second_moment.reshape(1, shard_rows),
    )
    return new_table.T, new_first.T, new_second.reshape(shard_rows)


def solution(mesh):
    in_specs = (
        P(("row", "col"), None, None),
        P(("row", "col"), None, None),
        P(),
        P(),
        P(),
        P(),
        P("row", None, None),
        P("row"),
        P("row", "col"),
        P("row", "col"),
        P("row"),
        P("row"),
    )
    out_specs = (P("row", "col"), P("row", "col"), P("row"))
    return jax.shard_map(body, mesh=mesh, in_specs=in_specs, out_specs=out_specs, check_vma=False)
```
